32 devices in a mesh: dp: 8 (over y, x, core), ctx: 4 (over z).
Axes of the slice: x: 2, y: 2, z: 4, core: 2. Of those that a mesh axis runs over, the one named last changes fastest.
Arguments:
- stream: bfloat16 [8, 512, 3072], P('dp', 'ctx'), may hold values from -210 to 210
- mod_shift: bfloat16 [8, 3072], P('dp'), may hold values from -3 to 3
- mod_scale: bfloat16 [8, 3072], P('dp'), may hold values from -1.796875 to 1.796875
- qkv_weight: bfloat16 [3072, 6144], P(None, 'dp'), may hold values from -0.109375 to 0.109375
- q_gain: float32 [128], replicated, may hold values from 0.7 to 2.2
- k_gain: float32 [128], replicated, may hold values from 0.7 to 2.2
Outputs:
- attended: bfloat16 [8, 512, 2048], P('dp', 'ctx')
The draws below stay inside these ranges and needn't reach their ends.
All inputs are finite; a program needn't handle non-finite values.
Results may differ from the reference program's by a relative error of at most 0.0049.
Values may be sent and summed in bfloat16 or wider, within the bound.
A program may use at most 128 MiB of HBM per device.

```python
import math
import jax
import jax.numpy as jnp
from jax import lax

D = 3072
HD = 128
HEADS = 16
HW = 2048
CLIPS = 8
SEQ = 512


def draw_stream(key, part):
    key = jax.random.fold_in(key, 11)
    key_base, key_rows, key_cols, key_extra = jax.random.split(key, 4)
    shape = (CLIPS, SEQ, D)
    row_scale = jnp.exp(jax.random.uniform(key_rows, (CLIPS, SEQ, 1), jnp.float32, 0.0, math.log(10.0)))
    col_scale = jnp.exp(jax.random.uniform(key_cols, (1, 1, D), jnp.float32, math.log(0.3), math.log(3.0)))
    base = jnp.clip(jax.random.normal(key_base, shape, jnp.float32), -6.0, 6.0)
    offset = jnp.clip(jax.random.normal(key_extra, (CLIPS, SEQ, 1), jnp.float32), -6.0, 6.0)
    field = (base * col_scale + 0.5 * offset) * row_scale
    return field.astype(jnp.bfloat16)


def steps_of(rng, dims, pieces, smallest, top_value):
    def one(axis_at, shards_of):
        heights = jax.random.uniform(jax.random.fold_in(jax.random.fold_in(rng, 6), axis_at), (shards_of,), jnp.float32, smallest / len(pieces), top_value / len(pieces))
        return jnp.repeat(jnp.exp(heights), dims[axis_at] // shards_of).reshape((-1,) + (1,) * (len(dims) - axis_at - 1))

    level = one(*pieces[0])
    for cut in pieces[1:]:
        level = level * one(*cut)
    return level


def gaussian(key, dims, spread, most, pieces=(), held_as=jnp.bfloat16):
    array = spread * jax.random.normal(key, dims, jnp.float32)
    if pieces:
        array = array * steps_of(key, dims, pieces, -0.22, 0.18)
    return jnp.clip(array, -most, most).astype(held_as)


def setup_inputs(seed: int = 0) -> dict:
    splits = jax.random.split(jax.random.key(seed), 7)
    stream = draw_stream(jax.random.fold_in(splits[6], 71), 0)
    mod_shift = gaussian(splits[1], (CLIPS, D), 0.5, 3.0, ((0, 8),))
    mod_scale = gaussian(splits[2], (CLIPS, D), 0.3, 1.796875, ((0, 8),))
    qkv_weight = gaussian(splits[3], (D, 3 * HW), D ** -0.5, 0.109375, ((1, 8),))
    q_gain = jnp.clip(jnp.exp(jax.random.uniform(splits[4], (HD,), jnp.float32, math.log(0.7), math.log(2.2))), 0.7, 2.2)
    k_gain = jnp.clip(jnp.exp(jax.random.uniform(splits[5], (HD,), jnp.float32, math.log(0.7), math.log(2.2))), 0.7, 2.2)
    return dict(stream=stream, mod_shift=mod_shift, mod_scale=mod_scale, qkv_weight=qkv_weight, q_gain=q_gain, k_gain=k_gain)


def head_norm(values, gain):
    shaped = values.astype(jnp.float32).reshape(values.shape[0], HEADS, HD)
    scale = lax.rsqrt(lax.optimization_barrier(jnp.mean(shaped * shaped, axis=-1, keepdims=True)) + 1e-06)
    return (shaped * scale * gain).astype(jnp.bfloat16)

def reference(stream, mod_shift, mod_scale, qkv_weight, q_gain, k_gain):

    def one_clip(items):
        hidden, shift, scale = items
        embedded = hidden.astype(jnp.float32)
        mean = lax.optimization_barrier(jnp.mean(embedded, axis=-1, keepdims=True))
        centred = embedded - mean
        var = lax.optimization_barrier(jnp.mean(centred * centred, axis=-1, keepdims=True))
        normed = (centred * lax.rsqrt(var + 1e-06) * (1.0 + scale.astype(jnp.float32)) + shift.astype(jnp.float32)).astype(jnp.bfloat16)
        projected = jnp.dot(normed, qkv_weight, preferred_element_type=jnp.float32).astype(jnp.bfloat16)
        qnorm = head_norm(projected[:, :HW], q_gain)
        knorm = head_norm(projected[:, HW:2 * HW], k_gain)
        values = projected[:, 2 * HW:].reshape(SEQ, HEADS, HD)
        scores = jnp.einsum('qhd,khd->hqk', qnorm.astype(jnp.float32), knorm.astype(jnp.float32)) / math.sqrt(HD)
        weights = jnp.exp(scores)
        totals = lax.optimization_barrier(jnp.sum(weights, axis=-1))
        rounded = lax.optimization_barrier(weights.astype(jnp.bfloat16)).astype(jnp.float32)
        summed = jnp.einsum('hqk,khd->hqd', rounded, values.astype(jnp.float32))
        result = summed / totals[:, :, None]
        return jnp.transpose(result, (1, 0, 2)).reshape(SEQ, HW).astype(jnp.bfloat16)
    return lax.map(one_clip, (stream, mod_shift, mod_scale))
```

```python
import functools
import math

import jax
import jax.numpy as jnp
from jax import lax
from jax.experimental import pallas as pl
from jax.experimental.pallas import tpu as pltpu
from jax.sharding import PartitionSpec as P

HD = 128
HEADS = 16
HW = 2048
MESH = pl.DeviceIdType.MESH


def flip(index, mask):
    out = index
    bit = 1
    while bit <= mask:
        if mask & bit:
            out = out + bit - 2 * bit * ((index // bit) % 2)
        bit *= 2
    return out


def last_hop(role, half):
    if half == 0:
        return role.bit_length() - 1
    return (role & -role).bit_length() - 1


def kernel(
    dp, ctx, unit,
    stream_ref, shift_ref, scale_ref, weight_hbm, qg_ref, kg_ref,
    out_ref,
    toks, weight, proj, mine, heads, outs,
    w_sem, t_send, t_recv, p_send, m_recv, z_send, r_sem, o_send, o_recv,
):
    i = lax.axis_index("dp")
    z = lax.axis_index("ctx")
    rows = stream_ref.shape[1]
    chips = dp // 2
    bits = chips.bit_length() - 1
    half_rows = rows // 2
    cols = weight.shape[1]
    m = cols // unit
    width = HW // ctx
    sub = width // unit
    seq = rows * ctx

    load = pltpu.make_async_copy(weight_hbm, weight, w_sem)
    load.start()

    barrier = pltpu.get_barrier_semaphore()
    for q in range(1, dp):
        pl.semaphore_signal(barrier, inc=1, device_id={"dp": flip(i, q)}, device_id_type=MESH)
    for k in range(1, ctx):
        pl.semaphore_signal(
            barrier, inc=1, device_id={"ctx": lax.rem(z + k, ctx)}, device_id_type=MESH
        )

    gain = 1.0 + scale_ref[...].astype(jnp.float32)
    shift = shift_ref[...].astype(jnp.float32)

    def norm_rows(at, _):
        hid = stream_ref[0, pl.ds(at * 16, 16), :].astype(jnp.float32)
        mean = jnp.mean(hid, axis=-1, keepdims=True)
        cen = hid - mean
        var = jnp.mean(cen * cen, axis=-1, keepdims=True)
        toks[0, pl.ds(at * 16, 16), :] = (cen * lax.rsqrt(var + 1e-06) * gain + shift).astype(
            jnp.bfloat16
        )
        return 0

    t_sent = []

    def send_tok(role_from, to_mask, role_to, sib, half):
        n = len(t_sent)
        copy = pltpu.make_async_remote_copy(
            src_ref=toks.at[role_from, pl.ds(half * half_rows, half_rows), :],
            dst_ref=toks.at[role_to, pl.ds(sib * rows + half * half_rows, half_rows), :],
            send_sem=t_send.at[n],
            recv_sem=t_recv.at[role_to, sib, half],
            device_id={"dp": flip(i, to_mask)},
            device_id_type=MESH,
        )
        copy.start()
        t_sent.append(copy)

    def wait_tok(role, sib, half):
        part = toks.at[role, pl.ds(sib * rows + half * half_rows, half_rows), :]
        pltpu.make_async_copy(part, part, t_recv.at[role, sib, half]).wait()

    def pass_on(role, half):
        for bit in range(bits):
            to = role ^ (1 << bit)
            if role >> bit & 1:
                continue
            if role == 0 or last_hop(to, half) == bit:
                send_tok(role, 2 << bit, to, 0, half)
        send_tok(role, 1, role, 1, half)

    steps = half_rows // 16
    lax.fori_loop(0, steps, norm_rows, 0)
    pl.semaphore_wait(barrier, dp + ctx - 2)
    pass_on(0, 0)
    lax.fori_loop(steps, 2 * steps, norm_rows, 0)
    pass_on(0, 1)

    qg = qg_ref[...]
    kg = kg_ref[...]
    p_sent = []

    def project(role):
        def one(j, _):
            u = m * i + j
            kind = u // (ctx * sub)
            flat = jnp.dot(
                toks[role],
                weight[:, pl.ds(pl.multiple_of(j * unit, unit), unit)],
                preferred_element_type=jnp.float32,
            ).astype(jnp.bfloat16)
            head_gain = jnp.where(kind == 0, qg, kg)
            for h in range(unit // HD):
                raw = flat[:, h * HD : (h + 1) * HD]
                val = raw.astype(jnp.float32)
                inv = lax.rsqrt(jnp.mean(val * val, axis=-1, keepdims=True) + 1e-06)
                res = jnp.where(kind < 2, val * inv * head_gain, val).astype(jnp.bfloat16)
                proj[2 * role, j, :, h * HD : (h + 1) * HD] = res[:rows]
                proj[2 * role + 1, j, :, h * HD : (h + 1) * HD] = res[rows:]
            return 0

        lax.fori_loop(0, m, one, 0)
        for k in range(2):
            q = 2 * role + k
            dst = mine.at[pl.ds(m * i, m)]
            if q == 0:
                copy = pltpu.make_async_copy(proj.at[0], dst, m_recv.at[i])
                copy.start()
            else:
                copy = pltpu.make_async_remote_copy(
                    src_ref=proj.at[q],
                    dst_ref=dst,
                    send_sem=p_send.at[q],
                    recv_sem=m_recv.at[i],
                    device_id={"dp": flip(i, q)},
                    device_id_type=MESH,
                )
                copy.start()
                p_sent.append(copy)

    def z_copy(q, j):
        u = m * flip(i, q) + j
        kind = u // (ctx * sub)
        to = (u // sub) % ctx
        h = u % sub
        src = mine.at[u]
        dst = heads.at[h, kind, pl.ds(z * rows, rows), :]

        def local():
            return pltpu.make_async_copy(src, dst, r_sem.at[h])

        def remote():
            return pltpu.make_async_remote_copy(
                src_ref=src,
                dst_ref=dst,
                send_sem=z_send.at[q * m + j],
                recv_sem=r_sem.at[h],
                device_id={"ctx": to},
                device_id_type=MESH,
            )

        return to, local, remote

    def to_heads(role):
        for q in (2 * role, 2 * role + 1):
            src = flip(i, q)
            part = mine.at[pl.ds(m * src, m)]
            pltpu.make_async_copy(part, part, m_recv.at[src]).wait()
            for j in range(m):
                to, local, remote = z_copy(q, j)
                pl.when(to == z)(lambda: local().start())
                pl.when(to != z)(lambda: remote().start())

    def wait_sib(role):
        for half in range(2):
            wait_tok(role, 1, half)

    load.wait()
    wait_sib(0)
    project(0)
    levels = [[r for r in range(chips) if r.bit_count() == n] for n in range(1, bits + 1)]
    done = [0]
    for level in levels:
        order = [(r, half) for half in range(2) for r in level]
        if len(level) == 2:
            order = [(level[0], 0), (level[1], 1), (level[0], 1), (level[1], 0)]
        for r, half in order:
            wait_tok(r, 0, half)
            pass_on(r, half)
        for r in done:
            to_heads(r)
        for r in level:
            wait_sib(r)
            project(r)
        done = level
    for r in done:
        to_heads(r)

    for h in range(sub):
        pltpu.make_async_copy(heads.at[h], heads.at[h], r_sem.at[h]).wait()

    root = 1.0 / math.sqrt(HD)
    o_sent = []
    for k in list(range(1, ctx)) + [0]:
        t = lax.rem(z + k, ctx)
        at = pl.ds(pl.multiple_of(t * rows, rows), rows)
        for h in range(sub):
            for p in range(unit // HD):
                lanes = slice(p * HD, (p + 1) * HD)
                scores = lax.dot_general(
                    heads[h, 0, at, lanes],
                    heads[h, 1, :, lanes],
                    (((1,), (1,)), ((), ())),
                    preferred_element_type=jnp.float32,
                )
                weights = jnp.exp(scores * root)
                totals = jnp.sum(weights, axis=-1, keepdims=True)
                summed = jnp.dot(
                    weights.astype(jnp.bfloat16),
                    heads[h, 2, :, lanes],
                    preferred_element_type=jnp.float32,
                )
                outs[k, :, pl.ds(h * unit + p * HD, HD)] = (summed / totals).astype(jnp.bfloat16)
        dst = out_ref.at[0, :, pl.ds(pl.multiple_of(z * width, width), width)]
        if k:
            copy = pltpu.make_async_remote_copy(
                src_ref=outs.at[k],
                dst_ref=dst,
                send_sem=o_send.at[k],
                recv_sem=o_recv.at[z],
                device_id={"ctx": t},
                device_id_type=MESH,
            )
            copy.start()
            o_sent.append(copy)
        else:
            pltpu.make_async_copy(outs.at[0], dst, o_recv.at[z]).start()

    for s in range(ctx):
        part = out_ref.at[0, :, pl.ds(s * width, width)]
        pltpu.make_async_copy(part, part, o_recv.at[s]).wait()
    for copy in t_sent + p_sent + o_sent:
        copy.wait_send()
    for q in range(dp):
        for j in range(m):
            to, _, remote = z_copy(q, j)
            pl.when(to != z)(lambda: remote().wait_send())


def shards(mesh, stream, mod_shift, mod_scale, qkv_weight, q_gain, k_gain):
    dp, ctx = mesh.shape["dp"], mesh.shape["ctx"]
    rows, depth = stream.shape[1:]
    cols = qkv_weight.shape[1]
    chips = dp // 2
    width = HW // ctx
    unit = math.gcd(cols, width)
    m = cols // unit
    sub = width // unit
    seq = rows * ctx
    dma = pltpu.SemaphoreType.DMA
    vmem = pl.BlockSpec(memory_space=pltpu.VMEM)
    return pl.pallas_call(
        functools.partial(kernel, dp, ctx, unit),
        out_shape=jax.ShapeDtypeStruct((1, rows, HW), jnp.bfloat16),
        in_specs=[vmem, vmem, vmem, pl.BlockSpec(memory_space=pl.ANY), vmem, vmem],
        out_specs=vmem,
        scratch_shapes=[
            pltpu.VMEM((chips, 2 * rows, depth), jnp.bfloat16),
            pltpu.VMEM((depth, cols), jnp.bfloat16),
            pltpu.VMEM((dp, m, rows, unit), jnp.bfloat16),
            pltpu.VMEM((dp * m, rows, unit), jnp.bfloat16),
            pltpu.VMEM((sub, 3, seq, unit), jnp.bfloat16),
            pltpu.VMEM((ctx, rows, width), jnp.bfloat16),
            dma,
            dma((4 * dp,)),
            dma((chips, 2, 2)),
            dma((dp,)),
            dma((dp,)),
            dma((dp * m,)),
            dma((sub,)),
            dma((ctx,)),
            dma((ctx,)),
        ],
        compiler_params=pltpu.CompilerParams(
            collective_id=0, has_side_effects=True, vmem_limit_bytes=56 * 1024 * 1024
        ),
    )(stream, mod_shift, mod_scale, qkv_weight, q_gain[None, :], k_gain[None, :])


def solution(mesh):
    placed = (P("dp", "ctx", None), P("dp", None), P("dp", None), P(None, "dp"), P(), P())
    return jax.shard_map(
        functools.partial(shards, mesh),
        mesh=mesh,
        in_specs=placed,
        out_specs=P("dp", "ctx", None),
        check_vma=False,
    )
```

```python
import functools
import math

import jax
import jax.numpy as jnp
from jax import lax
from jax.experimental import pallas as pl
from jax.experimental.pallas import tpu as pltpu
from jax.sharding import PartitionSpec as P

HD = 128
HEADS = 16
HW = 2048
MESH = pl.DeviceIdType.MESH
CHUNKS = 2


def flip(index, mask):
    out = index
    bit = 1
    while bit <= mask:
        if mask & bit:
            out = out + bit - 2 * bit * ((index // bit) % 2)
        bit *= 2
    return out


def last_hop(role, half):
    if half == 0:
        return role.bit_length() - 1
    return (role & -role).bit_length() - 1


def kernel(
    dp, ctx, unit,
    stream_ref, shift_ref, scale_ref, weight_hbm, qg_ref, kg_ref,
    out_ref,
    toks, weight, proj, mine, heads, outs,
    w_sem, t_send, t_recv, p_send, m_recv, z_send, r_sem, o_send, o_recv,
):
    i = lax.axis_index("dp")
    z = lax.axis_index("ctx")
    rows = stream_ref.shape[1]
    chips = dp // 2
    bits = chips.bit_length() - 1
    part = rows // CHUNKS
    piece = part // 2
    cols = weight.shape[1]
    m = cols // unit
    width = HW // ctx
    sub = width // unit
    seq = rows * ctx

    load = pltpu.make_async_copy(weight_hbm, weight, w_sem)
    load.start()

    barrier = pltpu.get_barrier_semaphore()
    for q in range(1, dp):
        pl.semaphore_signal(barrier, inc=1, device_id={"dp": flip(i, q)}, device_id_type=MESH)
    for k in range(1, ctx):
        pl.semaphore_signal(
            barrier, inc=1, device_id={"ctx": lax.rem(z + k, ctx)}, device_id_type=MESH
        )

    gain = 1.0 + scale_ref[...].astype(jnp.float32)
    shift = shift_ref[...].astype(jnp.float32)

    def norm_chunk(c):
        def norm_rows(at, _):
            hid = stream_ref[0, pl.ds(c * part + at * 16, 16), :].astype(jnp.float32)
            mean = jnp.mean(hid, axis=-1, keepdims=True)
            cen = hid - mean
            var = jnp.mean(cen * cen, axis=-1, keepdims=True)
            toks[c, 0, pl.ds(at * 16, 16), :] = (
                cen * lax.rsqrt(var + 1e-06) * gain + shift
            ).astype(jnp.bfloat16)
            return 0

        lax.fori_loop(0, part // 16, norm_rows, 0)

    t_sent = []

    def send_tok(c, role_from, to_mask, role_to, sib, half):
        n = len(t_sent)
        copy = pltpu.make_async_remote_copy(
            src_ref=toks.at[c, role_from, pl.ds(half * piece, piece), :],
            dst_ref=toks.at[c, role_to, pl.ds(sib * part + half * piece, piece), :],
            send_sem=t_send.at[n],
            recv_sem=t_recv.at[c, role_to, sib, half],
            device_id={"dp": flip(i, to_mask)},
            device_id_type=MESH,
        )
        copy.start()
        t_sent.append(copy)

    def wait_tok(c, role, sib, half):
        ref = toks.at[c, role, pl.ds(sib * part + half * piece, piece), :]
        pltpu.make_async_copy(ref, ref, t_recv.at[c, role, sib, half]).wait()

    def pass_on(c, role, half):
        for bit in range(bits):
            to = role ^ (1 << bit)
            if role >> bit & 1:
                continue
            if role == 0 or last_hop(to, half) == bit:
                send_tok(c, role, 2 << bit, to, 0, half)

    def pass_sib(c, role, half):
        send_tok(c, role, 1, role, 1, half)

    def send_direct(c):
        for bit in range(bits):
            for half in range(2):
                send_tok(c, 0, 2 << bit, 1 << bit, 0, half if bit % 2 == 0 else 1 - half)

    qg = qg_ref[...]
    kg = kg_ref[...]
    p_sent = []

    def project(c, role):
        def one(j, _):
            u = m * i + j
            kind = u // (ctx * sub)
            flat = jnp.dot(
                toks[c, role],
                weight[:, pl.ds(pl.multiple_of(j * unit, unit), unit)],
                preferred_element_type=jnp.float32,
            ).astype(jnp.bfloat16)
            head_gain = jnp.where(kind == 0, qg, kg)
            for h in range(unit // HD):
                raw = flat[:, h * HD : (h + 1) * HD]
                val = raw.astype(jnp.float32)
                inv = lax.rsqrt(jnp.mean(val * val, axis=-1, keepdims=True) + 1e-06)
                res = jnp.where(kind < 2, val * inv * head_gain, val).astype(jnp.bfloat16)
                proj[c, 2 * role, j, :, h * HD : (h + 1) * HD] = res[:part]
                proj[c, 2 * role + 1, j, :, h * HD : (h + 1) * HD] = res[part:]
            return 0

        lax.fori_loop(0, m, one, 0)
        for k in range(2):
            q = 2 * role + k
            dst = mine.at[c, pl.ds(m * i, m)]
            if q == 0:
                pltpu.make_async_copy(proj.at[c, 0], dst, m_recv.at[c, i]).start()
            else:
                copy = pltpu.make_async_remote_copy(
                    src_ref=proj.at[c, q],
                    dst_ref=dst,
                    send_sem=p_send.at[c, q],
                    recv_sem=m_recv.at[c, i],
                    device_id={"dp": flip(i, q)},
                    device_id_type=MESH,
                )
                copy.start()
                p_sent.append(copy)

    def z_copy(c, q, j):
        u = m * flip(i, q) + j
        kind = u // (ctx * sub)
        to = (u // sub) % ctx
        h = u % sub
        src = mine.at[c, u]
        dst = heads.at[h, kind, pl.ds(z * rows + c * part, part), :]

        def local():
            return pltpu.make_async_copy(src, dst, r_sem.at[h])

        def remote():
            return pltpu.make_async_remote_copy(
                src_ref=src,
                dst_ref=dst,
                send_sem=z_send.at[c, q * m + j],
                recv_sem=r_sem.at[h],
                device_id={"ctx": to},
                device_id_type=MESH,
            )

        return to, local, remote

    def to_heads(c, role):
        for q in (2 * role, 2 * role + 1):
            src = flip(i, q)
            ref = mine.at[c, pl.ds(m * src, m)]
            pltpu.make_async_copy(ref, ref, m_recv.at[c, src]).wait()
            for j in range(m):
                to, local, remote = z_copy(c, q, j)
                pl.when(to == z)(lambda: local().start())
                pl.when(to != z)(lambda: remote().start())

    def wait_sib(c, role):
        for half in range(2):
            wait_tok(c, role, 1, half)

    norm_chunk(0)
    pl.semaphore_wait(barrier, dp + ctx - 2)
    send_direct(0)
    for c in range(CHUNKS):
        if c:
            norm_chunk(c)
        for half in range(2):
            pass_sib(c, 0, half)
    load.wait()
    for c in range(CHUNKS):
        wait_sib(c, 0)
        project(c, 0)
    for c in range(CHUNKS):
        to_heads(c, 0)
    levels = [[r for r in range(chips) if r.bit_count() == n] for n in range(1, bits + 1)]
    done = []
    for c in range(CHUNKS):
        for at, level in enumerate(levels):
            order = [(r, half) for half in range(2) for r in level]
            if len(level) == 2:
                order = [(level[0], 0), (level[1], 1), (level[0], 1), (level[1], 0)]
            for r, half in order:
                wait_tok(c, r, 0, half)
                pass_on(c, r, half)
                pass_sib(c, r, half)
            if at == 0 and c + 1 < CHUNKS:
                send_direct(c + 1)
            for d in done:
                to_heads(*d)
            done = []
            for r in level:
                wait_sib(c, r)
                project(c, r)
                done.append((c, r))
    for d in done:
        to_heads(*d)

    for h in range(sub):
        pltpu.make_async_copy(heads.at[h], heads.at[h], r_sem.at[h]).wait()

    root = 1.0 / math.sqrt(HD)
    o_sent = []
    for k in list(range(1, ctx)) + [0]:
        t = lax.rem(z + k, ctx)
        at = pl.ds(pl.multiple_of(t * rows, rows), rows)
        for h in range(sub):
            for p in range(unit // HD):
                lanes = slice(p * HD, (p + 1) * HD)
                scores = lax.dot_general(
                    heads[h, 0, at, lanes],
                    heads[h, 1, :, lanes],
                    (((1,), (1,)), ((), ())),
                    preferred_element_type=jnp.float32,
                )
                weights = jnp.exp(scores * root)
                totals = jnp.sum(weights, axis=-1, keepdims=True)
                summed = jnp.dot(
                    weights.astype(jnp.bfloat16),
                    heads[h, 2, :, lanes],
                    preferred_element_type=jnp.float32,
                )
                outs[k, :, pl.ds(h * unit + p * HD, HD)] = (summed / totals).astype(jnp.bfloat16)
        dst = out_ref.at[0, :, pl.ds(pl.multiple_of(z * width, width), width)]
        if k:
            copy = pltpu.make_async_remote_copy(
                src_ref=outs.at[k],
                dst_ref=dst,
                send_sem=o_send.at[k],
                recv_sem=o_recv.at[z],
                device_id={"ctx": t},
                device_id_type=MESH,
            )
            copy.start()
            o_sent.append(copy)
        else:
            pltpu.make_async_copy(outs.at[0], dst, o_recv.at[z]).start()

    for s in range(ctx):
        ref = out_ref.at[0, :, pl.ds(s * width, width)]
        pltpu.make_async_copy(ref, ref, o_recv.at[s]).wait()
    for copy in t_sent + p_sent + o_sent:
        copy.wait_send()
    for c in range(CHUNKS):
        for q in range(dp):
            for j in range(m):
                to, _, remote = z_copy(c, q, j)
                pl.when(to != z)(lambda: remote().wait_send())


def shards(mesh, stream, mod_shift, mod_scale, qkv_weight, q_gain, k_gain):
    dp, ctx = mesh.shape["dp"], mesh.shape["ctx"]
    rows, depth = stream.shape[1:]
    cols = qkv_weight.shape[1]
    part = rows // CHUNKS
    chips = dp // 2
    width = HW // ctx
    unit = math.gcd(cols, width)
    m = cols // unit
    sub = width // unit
    seq = rows * ctx
    dma = pltpu.SemaphoreType.DMA
    vmem = pl.BlockSpec(memory_space=pltpu.VMEM)
    return pl.pallas_call(
        functools.partial(kernel, dp, ctx, unit),
        out_shape=jax.ShapeDtypeStruct((1, rows, HW), jnp.bfloat16),
        in_specs=[vmem, vmem, vmem, pl.BlockSpec(memory_space=pl.ANY), vmem, vmem],
        out_specs=vmem,
        scratch_shapes=[
            pltpu.VMEM((CHUNKS, chips, 2 * part, depth), jnp.bfloat16),
            pltpu.VMEM((depth, cols), jnp.bfloat16),
            pltpu.VMEM((CHUNKS, dp, m, part, unit), jnp.bfloat16),
            pltpu.VMEM((CHUNKS, dp * m, part, unit), jnp.bfloat16),
            pltpu.VMEM((sub, 3, seq, unit), jnp.bfloat16),
            pltpu.VMEM((ctx, rows, width), jnp.bfloat16),
            dma,
            dma((4 * dp * CHUNKS,)),
            dma((CHUNKS, chips, 2, 2)),
            dma((CHUNKS, dp)),
            dma((CHUNKS, dp)),
            dma((CHUNKS, dp * m)),
            dma((sub,)),
            dma((ctx,)),
            dma((ctx,)),
        ],
        compiler_params=pltpu.CompilerParams(
            collective_id=0, has_side_effects=True, vmem_limit_bytes=56 * 1024 * 1024
        ),
    )(stream, mod_shift, mod_scale, qkv_weight, q_gain[None, :], k_gain[None, :])


def solution(mesh):
    placed = (P("dp", "ctx", None), P("dp", None), P("dp", None), P(None, "dp"), P(), P())
    return jax.shard_map(
        functools.partial(shards, mesh),
        mesh=mesh,
        in_specs=placed,
        out_specs=P("dp", "ctx", None),
        check_vma=False,
    )
```

```python
import functools
import math

import jax
import jax.numpy as jnp
from jax import lax
from jax.experimental import pallas as pl
from jax.experimental.pallas import tpu as pltpu
from jax.sharding import PartitionSpec as P

HD = 128
HEADS = 16
HW = 2048
MESH = pl.DeviceIdType.MESH
CHUNKS = 2


def flip(index, mask):
    out = index
    bit = 1
    while bit <= mask:
        if mask & bit:
            out = out + bit - 2 * bit * ((index // bit) % 2)
        bit *= 2
    return out


def last_hop(role, half):
    if half == 0:
        return role.bit_length() - 1
    return (role & -role).bit_length() - 1


def kernel(
    dp, ctx, unit,
    stream_ref, shift_ref, scale_ref, weight_hbm, qg_ref, kg_ref,
    out_ref,
    toks, weight, proj, mine, heads, outs,
    w_sem, t_send, t_recv, p_send, m_recv, z_send, r_sem, o_send, o_recv,
):
    i = lax.axis_index("dp")
    z = lax.axis_index("ctx")
    rows = stream_ref.shape[1]
    chips = dp // 2
    bits = chips.bit_length() - 1
    part = rows // CHUNKS
    piece = part // 2
    cols = weight.shape[1]
    m = cols // unit
    width = HW // ctx
    sub = width // unit
    seq = rows * ctx

    load = pltpu.make_async_copy(weight_hbm, weight, w_sem)
    load.start()

    barrier = pltpu.get_barrier_semaphore()
    for q in range(1, dp):
        pl.semaphore_signal(barrier, inc=1, device_id={"dp": flip(i, q)}, device_id_type=MESH)
    for k in range(1, ctx):
        pl.semaphore_signal(
            barrier, inc=1, device_id={"ctx": lax.rem(z + k, ctx)}, device_id_type=MESH
        )

    gain = 1.0 + scale_ref[...].astype(jnp.float32)
    shift = shift_ref[...].astype(jnp.float32)

    def norm_chunk(c):
        def norm_rows(at, _):
            hid = stream_ref[0, pl.ds(c * part + at * 16, 16), :].astype(jnp.float32)
            mean = jnp.mean(hid, axis=-1, keepdims=True)
            cen = hid - mean
            var = jnp.mean(cen * cen, axis=-1, keepdims=True)
            toks[c, 0, pl.ds(at * 16, 16), :] = (
                cen * lax.rsqrt(var + 1e-06) * gain + shift
            ).astype(jnp.bfloat16)
            return 0

        lax.fori_loop(0, part // 16, norm_rows, 0)

    t_sent = []

    def send_tok(c, role_from, to_mask, role_to, sib, half):
        n = len(t_sent)
        copy = pltpu.make_async_remote_copy(
            src_ref=toks.at[c, role_from, pl.ds(half * piece, piece), :],
            dst_ref=toks.at[c, role_to, pl.ds(sib * part + half * piece, piece), :],
            send_sem=t_send.at[n],
            recv_sem=t_recv.at[c, role_to, sib, half],
            device_id={"dp": flip(i, to_mask)},
            device_id_type=MESH,
        )
        copy.start()
        t_sent.append(copy)

    def wait_tok(c, role, sib, half):
        ref = toks.at[c, role, pl.ds(sib * part + half * piece, piece), :]
        pltpu.make_async_copy(ref, ref, t_recv.at[c, role, sib, half]).wait()

    def pass_on(c, role, half):
        for bit in range(bits):
            to = role ^ (1 << bit)
            if role >> bit & 1:
                continue
            if role == 0 or last_hop(to, half) == bit:
                send_tok(c, role, 2 << bit, to, 0, half)

    def pass_sib(c, role, half):
        send_tok(c, role, 1, role, 1, half)

    def send_direct(c):
        for bit in range(bits):
            for half in range(2):
                send_tok(c, 0, 2 << bit, 1 << bit, 0, half if bit % 2 == 0 else 1 - half)

    qg = qg_ref[...]
    kg = kg_ref[...]
    p_sent = []

    def project(c, role):
        def one(j, _):
            u = m * i + j
            kind = u // (ctx * sub)
            flat = jnp.dot(
                toks[c, role],
                weight[:, pl.ds(pl.multiple_of(j * unit, unit), unit)],
                preferred_element_type=jnp.float32,
            ).astype(jnp.bfloat16)
            head_gain = jnp.where(kind == 0, qg, kg)
            for h in range(unit // HD):
                raw = flat[:, h * HD : (h + 1) * HD]
                val = raw.astype(jnp.float32)
                inv = lax.rsqrt(jnp.mean(val * val, axis=-1, keepdims=True) + 1e-06)
                res = jnp.where(kind < 2, val * inv * head_gain, val).astype(jnp.bfloat16)
                proj[c, 2 * role, j, :, h * HD : (h + 1) * HD] = res[:part]
                proj[c, 2 * role + 1, j, :, h * HD : (h + 1) * HD] = res[part:]
            return 0

        lax.fori_loop(0, m, one, 0)
        for k in range(2):
            q = 2 * role + k
            dst = mine.at[c, pl.ds(m * i, m)]
            if q == 0:
                pltpu.make_async_copy(proj.at[c, 0], dst, m_recv.at[c, i]).start()
            else:
                copy = pltpu.make_async_remote_copy(
                    src_ref=proj.at[c, q],
                    dst_ref=dst,
                    send_sem=p_send.at[c, q],
                    recv_sem=m_recv.at[c, i],
                    device_id={"dp": flip(i, q)},
                    device_id_type=MESH,
                )
                copy.start()
                p_sent.append(copy)

    def z_copy(c, q, j):
        u = m * flip(i, q) + j
        kind = u // (ctx * sub)
        to = (u // sub) % ctx
        h = u % sub
        src = mine.at[c, u]
        dst = heads.at[h, kind, pl.ds(z * rows + c * part, part), :]

        def local():
            return pltpu.make_async_copy(src, dst, r_sem.at[h])

        def remote():
            return pltpu.make_async_remote_copy(
                src_ref=src,
                dst_ref=dst,
                send_sem=z_send.at[c, q * m + j],
                recv_sem=r_sem.at[h],
                device_id={"ctx": to},
                device_id_type=MESH,
            )

        return to, local, remote

    def to_heads(c, role):
        for q in (2 * role, 2 * role + 1):
            src = flip(i, q)
            ref = mine.at[c, pl.ds(m * src, m)]
            pltpu.make_async_copy(ref, ref, m_recv.at[c, src]).wait()
            for j in range(m):
                to, local, remote = z_copy(c, q, j)
                pl.when(to == z)(lambda: local().start())
                pl.when(to != z)(lambda: remote().start())

    def wait_sib(c, role):
        for half in range(2):
            wait_tok(c, role, 1, half)

    for c in range(CHUNKS):
        norm_chunk(c)
    pl.semaphore_wait(barrier, dp + ctx - 2)
    send_direct(0)
    for c in range(CHUNKS):
        for half in range(2):
            pass_sib(c, 0, half)
    load.wait()
    for c in range(CHUNKS):
        wait_sib(c, 0)
        project(c, 0)
    for c in range(CHUNKS):
        to_heads(c, 0)
    levels = [[r for r in range(chips) if r.bit_count() == n] for n in range(1, bits + 1)]
    done = []
    for c in range(CHUNKS):
        for at, level in enumerate(levels):
            order = [(r, half) for half in range(2) for r in level]
            if len(level) == 2:
                order = [(level[0], 0), (level[1], 1), (level[0], 1), (level[1], 0)]
            for r, half in order:
                wait_tok(c, r, 0, half)
                pass_on(c, r, half)
                pass_sib(c, r, half)
            if at == 0 and c + 1 < CHUNKS:
                send_direct(c + 1)
            for r in level:
                wait_sib(c, r)
                project(c, r)
            for d in done:
                to_heads(*d)
            done = [(c, r) for r in level]
    for d in done:
        to_heads(*d)

    for h in range(sub):
        pltpu.make_async_copy(heads.at[h], heads.at[h], r_sem.at[h]).wait()

    root = 1.0 / math.sqrt(HD)
    o_sent = []
    for k in list(range(1, ctx)) + [0]:
        t = lax.rem(z + k, ctx)
        at = pl.ds(pl.multiple_of(t * rows, rows), rows)
        for h in range(sub):
            for p in range(unit // HD):
                lanes = slice(p * HD, (p + 1) * HD)
                scores = lax.dot_general(
                    heads[h, 0, at, lanes],
                    heads[h, 1, :, lanes],
                    (((1,), (1,)), ((), ())),
                    preferred_element_type=jnp.float32,
                )
                weights = jnp.exp(scores * root)
                totals = jnp.sum(weights, axis=-1, keepdims=True)
                summed = jnp.dot(
                    weights.astype(jnp.bfloat16),
                    heads[h, 2, :, lanes],
                    preferred_element_type=jnp.float32,
                )
                outs[k, :, pl.ds(h * unit + p * HD, HD)] = (summed / totals).astype(jnp.bfloat16)
        dst = out_ref.at[0, :, pl.ds(pl.multiple_of(z * width, width), width)]
        if k:
            copy = pltpu.make_async_remote_copy(
                src_ref=outs.at[k],
                dst_ref=dst,
                send_sem=o_send.at[k],
                recv_sem=o_recv.at[z],
                device_id={"ctx": t},
                device_id_type=MESH,
            )
            copy.start()
            o_sent.append(copy)
        else:
            pltpu.make_async_copy(outs.at[0], dst, o_recv.at[z]).start()

    for s in range(ctx):
        ref = out_ref.at[0, :, pl.ds(s * width, width)]
        pltpu.make_async_copy(ref, ref, o_recv.at[s]).wait()
    for copy in t_sent + p_sent + o_sent:
        copy.wait_send()
    for c in range(CHUNKS):
        for q in range(dp):
            for j in range(m):
                to, _, remote = z_copy(c, q, j)
                pl.when(to != z)(lambda: remote().wait_send())


def shards(mesh, stream, mod_shift, mod_scale, qkv_weight, q_gain, k_gain):
    dp, ctx = mesh.shape["dp"], mesh.shape["ctx"]
    rows, depth = stream.shape[1:]
    cols = qkv_weight.shape[1]
    part = rows // CHUNKS
    chips = dp // 2
    width = HW // ctx
    unit = math.gcd(cols, width)
    m = cols // unit
    sub = width // unit
    seq = rows * ctx
    dma = pltpu.SemaphoreType.DMA
    vmem = pl.BlockSpec(memory_space=pltpu.VMEM)
    return pl.pallas_call(
        functools.partial(kernel, dp, ctx, unit),
        out_shape=jax.ShapeDtypeStruct((1, rows, HW), jnp.bfloat16),
        in_specs=[vmem, vmem, vmem, pl.BlockSpec(memory_space=pl.ANY), vmem, vmem],
        out_specs=vmem,
        scratch_shapes=[
            pltpu.VMEM((CHUNKS, chips, 2 * part, depth), jnp.bfloat16),
            pltpu.VMEM((depth, cols), jnp.bfloat16),
            pltpu.VMEM((CHUNKS, dp, m, part, unit), jnp.bfloat16),
            pltpu.VMEM((CHUNKS, dp * m, part, unit), jnp.bfloat16),
            pltpu.VMEM((sub, 3, seq, unit), jnp.bfloat16),
            pltpu.VMEM((ctx, rows, width), jnp.bfloat16),
            dma,
            dma((4 * dp * CHUNKS,)),
            dma((CHUNKS, chips, 2, 2)),
            dma((CHUNKS, dp)),
            dma((CHUNKS, dp)),
            dma((CHUNKS, dp * m)),
            dma((sub,)),
            dma((ctx,)),
            dma((ctx,)),
        ],
        compiler_params=pltpu.CompilerParams(
            collective_id=0, has_side_effects=True, vmem_limit_bytes=56 * 1024 * 1024
        ),
    )(stream, mod_shift, mod_scale, qkv_weight, q_gain[None, :], k_gain[None, :])


def solution(mesh):
    placed = (P("dp", "ctx", None), P("dp", None), P("dp", None), P(None, "dp"), P(), P())
    return jax.shard_map(
        functools.partial(shards, mesh),
        mesh=mesh,
        in_specs=placed,
        out_specs=P("dp", "ctx", None),
        check_vma=False,
    )
```

```python
import functools
import math

import jax
import jax.numpy as jnp
from jax import lax
from jax.experimental import pallas as pl
from jax.experimental.pallas import tpu as pltpu
from jax.sharding import PartitionSpec as P

HD = 128
HEADS = 16
HW = 2048
MESH = pl.DeviceIdType.MESH
CHUNKS = 2


def flip(index, mask):
    out = index
    bit = 1
    while bit <= mask:
        if mask & bit:
            out = out + bit - 2 * bit * ((index // bit) % 2)
        bit *= 2
    return out


def last_hop(role, half):
    if half == 0:
        return role.bit_length() - 1
    return (role & -role).bit_length() - 1


def kernel(
    dp, ctx, unit,
    stream_ref, shift_ref, scale_ref, weight_hbm, qg_ref, kg_ref,
    out_ref,
    toks, weight, proj, mine, heads, outs,
    w_sem, t_send, t_recv, p_send, m_recv, z_send, r_sem, o_send, o_recv,
):
    i = lax.axis_index("dp")
    z = lax.axis_index("ctx")
    rows = stream_ref.shape[1]
    chips = dp // 2
    bits = chips.bit_length() - 1
    part = rows // CHUNKS
    piece = part // 2
    cols = weight.shape[1]
    m = cols // unit
    width = HW // ctx
    sub = width // unit
    seq = rows * ctx

    load = pltpu.make_async_copy(weight_hbm, weight, w_sem)
    load.start()

    barrier = pltpu.get_barrier_semaphore()
    for q in range(1, dp):
        pl.semaphore_signal(barrier, inc=1, device_id={"dp": flip(i, q)}, device_id_type=MESH)
    for k in range(1, ctx):
        pl.semaphore_signal(
            barrier, inc=1, device_id={"ctx": lax.rem(z + k, ctx)}, device_id_type=MESH
        )

    gain = 1.0 + scale_ref[...].astype(jnp.float32)
    shift = shift_ref[...].astype(jnp.float32)

    def norm_chunk(c):
        def norm_rows(at, _):
            hid = stream_ref[0, pl.ds(c * part + at * 16, 16), :].astype(jnp.float32)
            mean = jnp.mean(hid, axis=-1, keepdims=True)
            cen = hid - mean
            var = jnp.mean(cen * cen, axis=-1, keepdims=True)
            toks[c, 0, pl.ds(at * 16, 16), :] = (
                cen * lax.rsqrt(var + 1e-06) * gain + shift
            ).astype(jnp.bfloat16)
            return 0

        lax.fori_loop(0, part // 16, norm_rows, 0)

    t_sent = []

    def send_tok(c, role_from, to_mask, role_to, sib, half):
        n = len(t_sent)
        copy = pltpu.make_async_remote_copy(
            src_ref=toks.at[c, role_from, pl.ds(half * piece, piece), :],
            dst_ref=toks.at[c, role_to, pl.ds(sib * part + half * piece, piece), :],
            send_sem=t_send.at[n],
            recv_sem=t_recv.at[c, role_to, sib, half],
            device_id={"dp": flip(i, to_mask)},
            device_id_type=MESH,
        )
        copy.start()
        t_sent.append(copy)

    def wait_tok(c, role, sib, half):
        ref = toks.at[c, role, pl.ds(sib * part + half * piece, piece), :]
        pltpu.make_async_copy(ref, ref, t_recv.at[c, role, sib, half]).wait()

    def pass_on(c, role, half):
        for bit in range(bits):
            to = role ^ (1 << bit)
            if role >> bit & 1:
                continue
            if role == 0 or last_hop(to, half) == bit:
                send_tok(c, role, 2 << bit, to, 0, half)

    def pass_sib(c, role, half):
        send_tok(c, role, 1, role, 1, half)

    def send_direct(c):
        for bit in range(bits):
            for half in range(2):
                send_tok(c, 0, 2 << bit, 1 << bit, 0, half if bit % 2 == 0 else 1 - half)

    qg = qg_ref[...]
    kg = kg_ref[...]
    p_sent = []

    def project(c, role):
        def one(j, _):
            u = m * i + j
            kind = u // (ctx * sub)
            flat = jnp.dot(
                toks[c, role],
                weight[:, pl.ds(pl.multiple_of(j * unit, unit), unit)],
                preferred_element_type=jnp.float32,
            ).astype(jnp.bfloat16)
            head_gain = jnp.where(kind == 0, qg, kg)
            for h in range(unit // HD):
                raw = flat[:, h * HD : (h + 1) * HD]
                val = raw.astype(jnp.float32)
                inv = lax.rsqrt(jnp.mean(val * val, axis=-1, keepdims=True) + 1e-06)
                res = jnp.where(kind < 2, val * inv * head_gain, val).astype(jnp.bfloat16)
                proj[c, 2 * role, j, :, h * HD : (h + 1) * HD] = res[:part]
                proj[c, 2 * role + 1, j, :, h * HD : (h + 1) * HD] = res[part:]
            for q in (2 * role, 2 * role + 1):
                dst = mine.at[c, u]
                if q == 0:
                    pltpu.make_async_copy(proj.at[c, 0, j], dst, m_recv.at[c, i]).start()
                else:
                    back(q, proj.at[c, q, j], dst).start()
            return 0

        def back(q, src, dst):
            return pltpu.make_async_remote_copy(
                src_ref=src,
                dst_ref=dst,
                send_sem=p_send.at[c, q],
                recv_sem=m_recv.at[c, i],
                device_id={"dp": flip(i, q)},
                device_id_type=MESH,
            )

        lax.fori_loop(0, m, one, 0)
        for q in (2 * role, 2 * role + 1):
            if q:
                p_sent.append(back(q, proj.at[c, q], mine.at[c, pl.ds(m * i, m)]))

    def z_copy(c, q, j):
        u = m * flip(i, q) + j
        kind = u // (ctx * sub)
        to = (u // sub) % ctx
        h = u % sub
        src = mine.at[c, u]
        dst = heads.at[h, kind, pl.ds(z * rows + c * part, part), :]

        def local():
            return pltpu.make_async_copy(src, dst, r_sem.at[h])

        def remote():
            return pltpu.make_async_remote_copy(
                src_ref=src,
                dst_ref=dst,
                send_sem=z_send.at[c, q * m + j],
                recv_sem=r_sem.at[h],
                device_id={"ctx": to},
                device_id_type=MESH,
            )

        return to, local, remote

    def to_heads(c, role):
        for q in (2 * role, 2 * role + 1):
            src = flip(i, q)
            ref = mine.at[c, pl.ds(m * src, m)]
            pltpu.make_async_copy(ref, ref, m_recv.at[c, src]).wait()
            for j in range(m):
                to, local, remote = z_copy(c, q, j)
                pl.when(to == z)(lambda: local().start())
                pl.when(to != z)(lambda: remote().start())

    def wait_sib(c, role):
        for half in range(2):
            wait_tok(c, role, 1, half)

    for c in range(CHUNKS):
        norm_chunk(c)
    pl.semaphore_wait(barrier, dp + ctx - 2)
    send_direct(0)
    for c in range(CHUNKS):
        for half in range(2):
            pass_sib(c, 0, half)
    load.wait()
    for c in range(CHUNKS):
        wait_sib(c, 0)
        project(c, 0)
    for c in range(CHUNKS):
        to_heads(c, 0)
    levels = [[r for r in range(chips) if r.bit_count() == n] for n in range(1, bits + 1)]
    done = []
    for c in range(CHUNKS):
        for at, level in enumerate(levels):
            order = [(r, half) for half in range(2) for r in level]
            if len(level) == 2:
                order = [(level[0], 0), (level[1], 1), (level[0], 1), (level[1], 0)]
            for r, half in order:
                wait_tok(c, r, 0, half)
                pass_on(c, r, half)
                pass_sib(c, r, half)
            if at == 0 and c + 1 < CHUNKS:
                send_direct(c + 1)
            for r in level:
                wait_sib(c, r)
                project(c, r)
            for d in done:
                to_heads(*d)
            done = [(c, r) for r in level]
    for d in done:
        to_heads(*d)

    for h in range(sub):
        pltpu.make_async_copy(heads.at[h], heads.at[h], r_sem.at[h]).wait()

    root = 1.0 / math.sqrt(HD)
    o_sent = []
    for k in list(range(1, ctx)) + [0]:
        t = lax.rem(z + k, ctx)
        at = pl.ds(pl.multiple_of(t * rows, rows), rows)
        for h in range(sub):
            for p in range(unit // HD):
                lanes = slice(p * HD, (p + 1) * HD)
                scores = lax.dot_general(
                    heads[h, 0, at, lanes],
                    heads[h, 1, :, lanes],
                    (((1,), (1,)), ((), ())),
                    preferred_element_type=jnp.float32,
                )
                weights = jnp.exp(scores * root)
                totals = jnp.sum(weights, axis=-1, keepdims=True)
                summed = jnp.dot(
                    weights.astype(jnp.bfloat16),
                    heads[h, 2, :, lanes],
                    preferred_element_type=jnp.float32,
                )
                outs[k, :, pl.ds(h * unit + p * HD, HD)] = (summed / totals).astype(jnp.bfloat16)
        dst = out_ref.at[0, :, pl.ds(pl.multiple_of(z * width, width), width)]
        if k:
            copy = pltpu.make_async_remote_copy(
                src_ref=outs.at[k],
                dst_ref=dst,
                send_sem=o_send.at[k],
                recv_sem=o_recv.at[z],
                device_id={"ctx": t},
                device_id_type=MESH,
            )
            copy.start()
            o_sent.append(copy)
        else:
            pltpu.make_async_copy(outs.at[0], dst, o_recv.at[z]).start()

    for s in range(ctx):
        ref = out_ref.at[0, :, pl.ds(s * width, width)]
        pltpu.make_async_copy(ref, ref, o_recv.at[s]).wait()
    for copy in t_sent + p_sent + o_sent:
        copy.wait_send()
    for c in range(CHUNKS):
        for q in range(dp):
            for j in range(m):
                to, _, remote = z_copy(c, q, j)
                pl.when(to != z)(lambda: remote().wait_send())


def shards(mesh, stream, mod_shift, mod_scale, qkv_weight, q_gain, k_gain):
    dp, ctx = mesh.shape["dp"], mesh.shape["ctx"]
    rows, depth = stream.shape[1:]
    cols = qkv_weight.shape[1]
    part = rows // CHUNKS
    chips = dp // 2
    width = HW // ctx
    unit = math.gcd(cols, width)
    m = cols // unit
    sub = width // unit
    seq = rows * ctx
    dma = pltpu.SemaphoreType.DMA
    vmem = pl.BlockSpec(memory_space=pltpu.VMEM)
    return pl.pallas_call(
        functools.partial(kernel, dp, ctx, unit),
        out_shape=jax.ShapeDtypeStruct((1, rows, HW), jnp.bfloat16),
        in_specs=[vmem, vmem, vmem, pl.BlockSpec(memory_space=pl.ANY), vmem, vmem],
        out_specs=vmem,
        scratch_shapes=[
            pltpu.VMEM((CHUNKS, chips, 2 * part, depth), jnp.bfloat16),
            pltpu.VMEM((depth, cols), jnp.bfloat16),
            pltpu.VMEM((CHUNKS, dp, m, part, unit), jnp.bfloat16),
            pltpu.VMEM((CHUNKS, dp * m, part, unit), jnp.bfloat16),
            pltpu.VMEM((sub, 3, seq, unit), jnp.bfloat16),
            pltpu.VMEM((ctx, rows, width), jnp.bfloat16),
            dma,
            dma((4 * dp * CHUNKS,)),
            dma((CHUNKS, chips, 2, 2)),
            dma((CHUNKS, dp)),
            dma((CHUNKS, dp)),
            dma((CHUNKS, dp * m)),
            dma((sub,)),
            dma((ctx,)),
            dma((ctx,)),
        ],
        compiler_params=pltpu.CompilerParams(
            collective_id=0, has_side_effects=True, vmem_limit_bytes=56 * 1024 * 1024
        ),
    )(stream, mod_shift, mod_scale, qkv_weight, q_gain[None, :], k_gain[None, :])


def solution(mesh):
    placed = (P("dp", "ctx", None), P("dp", None), P("dp", None), P(None, "dp"), P(), P())
    return jax.shard_map(
        functools.partial(shards, mesh),
        mesh=mesh,
        in_specs=placed,
        out_specs=P("dp", "ctx", None),
        check_vma=False,
    )
```
